512 devices in a mesh: season: 16 (over z, core), farm: 32 (over x, y).
Axes of the slice: x: 4, y: 8, z: 8, core: 2. Of those that a mesh axis runs over, the one named last changes fastest.
Arguments:
- station_index: bfloat16 [32768, 10240], P('farm', 'season'), may hold values from -6 to 6
- strike_day: int32 [32768], P('farm'), may hold values from 0 to 63
- exit_day: int32 [32768], P('farm'), may hold values from 65 to 128
- farm_yield: bfloat16 [32768, 10240], P('farm', 'season'), as said below
- send_list: int32 [32, 32, 2], P('farm'), may hold values from 0 to 7, as said below
- pair_list: int32 [2048, 2], P('farm'), may hold values from 0 to 255, as said below
Outputs:
- gram: float32 [128, 2048, 128], P('season', 'farm')
The draws below stay inside these ranges and needn't reach their ends.
Inputs may be any that keep to these rules, and one draw needn't show every extreme that they name: `send_list`: each entry names a local station block of the source farm index; the 2 entries of one source and destination are distinct. `pair_list`: the rows of farm index d name, in the first column, farm blocks d * 8 to d * 8 + 7, and in the second a slot s = q * 2 + c whose place c is below the number of blocks source q relays to d; a farm index relays 2 blocks to itself, and 1 to 2 to each other one. `farm_yield`: finite yield proxies with a level and a drift over the days.
All inputs are finite; a program needn't handle non-finite values.
Results may differ from the reference program's by a relative error of at most 0.0032.
Values may be sent and summed in bfloat16 or wider, within the bound.
No kernel may reach another device: no remote copies, remote signals or barrier semaphores. Data moves between devices by JAX's collectives and lax.ppermute only.
A program may use at most 128 MiB of HBM per device.

```python
import math
import jax
import jax.numpy as jnp
from jax import lax

SEASON_DAYS = 128
FBLOCK = 128
SBLOCK = 128
SB_DEV = 8
FB_DEV = 8
CAP = 2
DAYS = 10240
STATIONS = 32768
FARMS = 32768
PAIRS_DEV = 64
PAIRS = 2048
N_FARM = 32


def relay_plan(key):
    key_count = jax.random.fold_in(key, 11)
    key_order = jax.random.fold_in(key, 12)
    key_slot = jax.random.fold_in(key, 13)
    key_farm = jax.random.fold_in(key, 14)
    counts = jax.random.randint(key_count, (N_FARM, N_FARM), 1, CAP + 1)
    diagonal_on = jnp.eye(N_FARM, dtype=jnp.int32)
    counts = jnp.where(diagonal_on > 0, CAP, counts).astype(jnp.int32)
    scores = jax.random.randint(key_order, (N_FARM, N_FARM, SB_DEV), 0, 1 << 20) * SB_DEV + jnp.arange(SB_DEV, dtype=jnp.int32)
    sent_blocks = jnp.argsort(scores, axis=-1)[:, :, :CAP].astype(jnp.int32)
    slot_used = jnp.arange(CAP, dtype=jnp.int32)[None, None, :] < counts[:, :, None]
    per_dest = jnp.transpose(slot_used, (1, 0, 2)).reshape(N_FARM, N_FARM * CAP).astype(jnp.int32)
    used_total = jnp.sum(per_dest, axis=1)
    slot_rank = jnp.cumsum(per_dest, axis=1) - 1
    random_rank = jax.random.randint(key_slot, (N_FARM, PAIRS_DEV), 0, used_total[:, None])
    pair_index = jnp.arange(PAIRS_DEV, dtype=jnp.int32)[None, :]
    pick_rank = jnp.where(pair_index < used_total[:, None], pair_index, random_rank)
    match_on = (per_dest[:, None, :] > 0) & (slot_rank[:, None, :] == pick_rank[:, :, None])
    slot_pick = jnp.argmax(match_on.astype(jnp.int32), axis=2).astype(jnp.int32)
    farm_pick = jax.random.randint(key_farm, (N_FARM, PAIRS_DEV), 0, FB_DEV) + jnp.arange(N_FARM, dtype=jnp.int32)[:, None] * FB_DEV
    pair_table = jnp.stack([farm_pick.astype(jnp.int32), slot_pick], axis=-1).reshape(PAIRS, 2)
    return (sent_blocks, pair_table)


def draw_send_list(key, part):
    sent_blocks, pair_table = relay_plan(key)
    return sent_blocks


def draw_pair_list(key, part):
    sent_blocks, pair_table = relay_plan(key)
    return pair_table


def draw_farm_yield(key, part):
    key = jax.random.fold_in(key, 7)
    key_level, key_trend, key_rows, key_days, key_noise = jax.random.split(key, 5)
    level = jax.random.uniform(key_level, (FARMS, 1), jnp.float32, 0.5, 1.5)
    trend = jax.random.uniform(key_trend, (FARMS, 1), jnp.float32, 1.0, 3.0)
    row_scale = jnp.exp(jax.random.uniform(key_rows, (FARMS, 1), jnp.float32, math.log(0.3), math.log(3.0)))
    day_scale = jnp.exp(jax.random.uniform(key_days, (1, DAYS), jnp.float32, math.log(0.5), math.log(5.0)))
    ramp = jnp.arange(DAYS, dtype=jnp.float32)[None, :] / DAYS
    noise = jax.random.normal(key_noise, (FARMS, DAYS), jnp.float32)
    values = level + trend * ramp + row_scale * day_scale * noise
    return values.astype(jnp.bfloat16)


def with_ends(drawn, stream_key, least, top_value):
    spot = [jax.random.randint(jax.random.fold_in(stream_key, axis), (), 0, length) for axis, length in enumerate(drawn.shape)]
    main_axis = drawn.shape.index(max(drawn.shape))
    next_to = spot[:main_axis] + [(spot[main_axis] + 1) % drawn.shape[main_axis]] + spot[main_axis + 1:]
    return drawn.at[tuple(spot)].set(least).at[tuple(next_to)].set(top_value)


def steps_of(rng, extent, cuts, low, largest):
    level, own = 1.0, jax.random.fold_in(rng, 6)
    for dim, shards_of in cuts:
        steps = jnp.exp(jax.random.uniform(jax.random.fold_in(own, dim), (shards_of,), jnp.float32, low / len(cuts), largest / len(cuts)))
        level = level * jnp.repeat(steps, extent[dim] // shards_of).reshape([-1 if axis == dim else 1 for axis in range(len(extent))])
    return level


def normal_values(stream_key, shape, width, reach, cuts=(), kind=jnp.bfloat16):
    gain = steps_of(stream_key, shape, cuts, -0.22, 0.18) if cuts else 1.0
    values = jax.random.normal(stream_key, shape, jnp.float32) * width * gain
    return jnp.minimum(jnp.maximum(values, -reach), reach).astype(kind)


def setup_inputs(seed: int = 0) -> dict:
    key_list = jax.random.split(jax.random.key(seed), 7)
    station_index = normal_values(key_list[0], (STATIONS, DAYS), 1.0, 6.0, ((0, 32), (1, 16)))
    strike_day = with_ends(jax.random.randint(key_list[1], (STATIONS,), 0, SEASON_DAYS // 2), jax.random.fold_in(key_list[1], 1), 0, (SEASON_DAYS // 2) - 1).astype(jnp.int32)
    exit_day = with_ends(jax.random.randint(key_list[2], (STATIONS,), SEASON_DAYS // 2 + 1, SEASON_DAYS + 1), jax.random.fold_in(key_list[2], 1), SEASON_DAYS // 2 + 1, SEASON_DAYS).astype(jnp.int32)
    farm_yield = draw_farm_yield(jax.random.fold_in(key_list[6], 71), 0)
    send_list = draw_send_list(jax.random.fold_in(key_list[6], 71), 0)
    pair_list = draw_pair_list(jax.random.fold_in(key_list[6], 71), 0)
    return {"station_index": station_index, "strike_day": strike_day, "exit_day": exit_day, "farm_yield": farm_yield, "send_list": send_list, "pair_list": pair_list}


def payout(series, strike_days, exit_days):
    row_total, day_total = series.shape
    shaped = series.reshape(row_total, day_total // SEASON_DAYS, SEASON_DAYS).astype(jnp.float32)
    day_index = jnp.arange(SEASON_DAYS, dtype=jnp.int32)[None, None, :]
    start_on = day_index >= strike_days[:, None, None]
    masked = jnp.where(start_on, shaped, jnp.zeros_like(shaped))
    running = jnp.cumsum(masked, axis=2)
    window_on = start_on & (day_index < exit_days[:, None, None])
    value = jax.nn.softplus(0.3 * running + shaped)
    result = jnp.where(window_on, value, jnp.zeros_like(value))
    return result.astype(jnp.bfloat16).reshape(row_total, day_total)

def payout_block(block_args):
    series, strike_days, exit_days = block_args
    return payout(series, strike_days, exit_days)

def center_block(block):
    values = block.astype(jnp.float32)
    center = lax.optimization_barrier(jnp.mean(values, axis=1, keepdims=True))
    offset = values - center
    spread = lax.optimization_barrier(jnp.mean(offset * offset, axis=1, keepdims=True))
    return (offset * lax.rsqrt(spread + 1e-05)).astype(jnp.bfloat16)

def reference(station_index, strike_day, exit_day, farm_yield, send_list, pair_list):
    station_blocks = STATIONS // SBLOCK
    farm_blocks = FARMS // FBLOCK
    paid = lax.map(payout_block, (station_index.reshape(station_blocks, SBLOCK, DAYS), strike_day.reshape(station_blocks, SBLOCK), exit_day.reshape(station_blocks, SBLOCK)))
    scaled = lax.map(center_block, farm_yield.reshape(farm_blocks, FBLOCK, DAYS))
    table = pair_list.reshape(N_FARM, PAIRS_DEV, 2)
    dest = jnp.arange(N_FARM, dtype=jnp.int32)[:, None]
    slot_pick = table[:, :, 1]
    source = (slot_pick // CAP).astype(jnp.int32)
    place = (slot_pick % CAP).astype(jnp.int32)
    station_of = (source * SB_DEV + send_list[source, dest, place]).astype(jnp.int32)
    farm_of = table[:, :, 0].astype(jnp.int32)
    factor = float(DAYS) ** (-0.5)

    def per_device(device_args):
        farm_ids, station_ids = device_args
        left_side = scaled[farm_ids].astype(jnp.float32)
        right_side = paid[station_ids].astype(jnp.float32)
        product = jnp.einsum('pfd,psd->fps', left_side, right_side, precision=lax.Precision.HIGHEST)
        return product * factor
    grams = lax.map(per_device, (farm_of, station_of))
    return grams.transpose(1, 0, 2, 3).reshape(FBLOCK, PAIRS, SBLOCK)
```

```python
import jax
import jax.numpy as jnp
from jax import lax
from jax.experimental import pallas as pl
from jax.experimental.pallas import tpu as pltpu
from jax.sharding import PartitionSpec as P

DAY = 128
BLK = 128
NX, NY, NZ = 4, 8, 8
FB_DEV = 8
GATE = 2
STEPS = (2, 1, 3)
VMEM_CAP = 48 * 1024 * 1024


def y_shift(k):
    return [(x * NY + y, x * NY + (y + k) % NY) for x in range(NX) for y in range(NY)]


ROWS = [[x * NY + y for y in range(NY)] for x in range(NX)]


def x_shift(k):
    return [(x * NY + y, ((x + k) % NX) * NY + y) for x in range(NX) for y in range(NY)]


def z_shift(k):
    return [(z * 2 + c, ((z + k) % NZ) * 2 + c) for z in range(NZ) for c in range(2)]


CORE_SWAP = [(i, i ^ 1) for i in range(2 * NZ)]


def payout_kernel(first, strike_ref, exit_ref, series_ref, out_ref):
    b = pl.program_id(0) + first
    tau = lax.broadcasted_iota(jnp.int32, (BLK, DAY), 1)
    row = lax.broadcasted_iota(jnp.int32, (BLK, DAY), 0)
    upper = jnp.where(row <= tau, 1.0, 0.0).astype(jnp.bfloat16)
    tau = tau.astype(jnp.float32)

    def column(ref):
        line = ref[pl.ds(b, 1), :].astype(jnp.float32)
        return jnp.transpose(jnp.broadcast_to(line, (BLK, BLK)))

    start_on = tau >= column(strike_ref)
    window_on = start_on & (tau < column(exit_ref))
    for s in range(out_ref.shape[2] // DAY):
        days = slice(s * DAY, (s + 1) * DAY)
        x = series_ref[:, days].astype(jnp.float32)
        masked = jnp.where(start_on, x, 0.0).astype(jnp.bfloat16)
        running = jnp.dot(masked, upper, preferred_element_type=jnp.float32)
        v = 0.3 * running + x
        value = jnp.maximum(v, 0.0) + jnp.log1p(jnp.exp(-jnp.abs(v)))
        out_ref[0, :, days] = jnp.where(window_on, value, 0.0).astype(jnp.bfloat16)


def payouts(series, strike, leave, first, count, before=None, gate=None):
    rows, days = series.shape
    blocks = rows // BLK
    lines = pl.BlockSpec((blocks, BLK), lambda b: (0, 0))
    operands = [strike.reshape(blocks, BLK), leave.reshape(blocks, BLK), series]
    specs = [lines, lines, pl.BlockSpec((BLK, days), lambda b: (b + first, 0))]
    alias = {}
    if before is not None:
        operands += [before, gate]
        specs += [pl.BlockSpec(memory_space=pl.ANY)] * 2
        alias = {3: 0}
    return pl.pallas_call(
        lambda *refs: payout_kernel(first, *refs[:3], refs[-1]),
        grid=(count,),
        out_shape=jax.ShapeDtypeStruct((blocks, BLK, days), jnp.bfloat16),
        in_specs=specs,
        out_specs=pl.BlockSpec((1, BLK, days), lambda b: (b + first, 0, 0)),
        input_output_aliases=alias,
        name="payouts",
    )(*operands)


def pick_kernel(backs, table_ref, place_ref, *refs):
    outs, held, sems = refs[-2 - len(STEPS):-2], refs[-2], refs[-1]
    half = BLK // 2
    copies = []
    for step, out in zip(STEPS, outs):
        x = lax.rem(place_ref[0] + step, NX)
        for i, back in enumerate(backs):
            line = 0 if back is None else lax.rem(place_ref[1] + NY - back, NY)
            for c in range(2):
                block = table_ref[line, x * 2 + c]
                n, where = len(copies), out.at[2 * i + c]
                if refs[0].shape[1] == BLK:
                    copies.append((refs[i].at[block], where, n, 0, BLK))
                else:
                    for h in range(2):
                        copies.append((refs[h].at[block], where.at[pl.ds(h * half, half)], n, h * half, half))
    inward, outward = [], []
    for n, (src, dst, at, low, rows) in enumerate(copies):
        copy = pltpu.make_async_copy(src, held.at[at, pl.ds(low, rows)], sems.at[0, n])
        copy.start()
        inward.append(copy)
    for n, (src, dst, at, low, rows) in enumerate(copies):
        inward[n].wait()
        copy = pltpu.make_async_copy(held.at[at, pl.ds(low, rows)], dst, sems.at[1, n])
        copy.start()
        outward.append(copy)
    for copy in outward:
        copy.wait()


def picks(table, place, sources, backs, gate=()):
    days = sources[0].shape[-1]
    count = 2 * len(backs)
    number = count * len(STEPS) * (1 if sources[0].shape[1] == BLK else 2)
    operands = list(sources) + list(gate)
    return pl.pallas_call(
        lambda *refs: pick_kernel(backs, *refs),
        out_shape=[jax.ShapeDtypeStruct((count, BLK, days), jnp.bfloat16)] * len(STEPS),
        in_specs=[pl.BlockSpec(memory_space=pltpu.SMEM)] * 2 + [pl.BlockSpec(memory_space=pl.ANY)] * len(operands),
        out_specs=[pl.BlockSpec(memory_space=pl.ANY)] * len(STEPS),
        scratch_shapes=[pltpu.VMEM((number, BLK, days), jnp.bfloat16), pltpu.SemaphoreType.DMA((2, number))],
        compiler_params=pltpu.CompilerParams(vmem_limit_bytes=VMEM_CAP),
        cost_estimate=pl.CostEstimate(flops=0, bytes_accessed=number * BLK * days * 4, transcendentals=0),
        name="picks",
    )(table, place, *operands)


def gram_kernel(factor, table_ref, place_ref, pair_ref, farm_ref, *refs):
    held, relayed = refs[:9], refs[9:24]
    keep_ref, send_ref, slots, sems = refs[24:]
    x, y, z, core = place_ref[0], place_ref[1], place_ref[2], place_ref[3]
    copies = []
    half = BLK // 2
    for at, back in enumerate((0, 1, 7, 2, 6, 3, 5, 4)):
        for c in range(2):
            block = table_ref[lax.rem(y + NY - back, NY), x * 2 + c]
            if at < 7:
                copies.append((held[at].at[block], slots.at[0, 2 * at + c]))
            else:
                for h in range(2):
                    copies.append((held[7 + h].at[block], slots.at[0, 2 * at + c, pl.ds(h * half, half)]))
    for i, step in enumerate(STEPS):
        at = 0
        for ref in relayed[i::len(STEPS)]:
            n = ref.shape[0]
            copies.append((ref, slots.at[step, pl.ds(at, n)]))
            at += n
    started = []
    for n, (src, dst) in enumerate(copies):
        copy = pltpu.make_async_copy(src, dst, sems.at[n])
        copy.start()
        started.append(copy)
    for copy in started:
        copy.wait()

    first = (x * NY + y) * FB_DEV

    def one(p):
        farm = pair_ref[p, 0] - first
        slot = pair_ref[p, 1]
        source, c = slot // 2, lax.rem(slot, 2)
        sx, sy = source // NY, lax.rem(source, NY)
        dy = lax.rem(y - sy + NY, NY)
        place = jnp.where(dy == 0, 0, jnp.where(dy < 4, 2 * dy - 1, jnp.where(dy == 4, 7, 2 * (NY - dy))))
        product = lax.dot_general(
            farm_ref[farm], slots[lax.rem(x - sx + NX, NX), place * 2 + c], (((1,), (1,)), ((), ())), preferred_element_type=jnp.float32
        ) * factor
        for target in range(NZ):
            near_rows = product[target * 16: target * 16 + 8]
            far_rows = product[target * 16 + 8: target * 16 + 16]
            d = lax.rem(target - z + NZ, NZ)
            keep_ref[d, p] = jnp.where(core == 0, near_rows, far_rows)
            send_ref[d, p] = jnp.where(core == 0, far_rows, near_rows)

    pl.loop(0, pair_ref.shape[0], unroll=4)(one)


def grams(factor, table, place, pairs, farms, stations):
    days = farms.shape[-1]
    count = pairs.shape[0]
    shape = jax.ShapeDtypeStruct((NZ, count, 8, BLK), jnp.float32)
    vmem = pl.BlockSpec(memory_space=pltpu.VMEM)
    return pl.pallas_call(
        lambda *refs: gram_kernel(factor, *refs),
        out_shape=[shape] * 2,
        in_specs=[pl.BlockSpec(memory_space=pltpu.SMEM)] * 3 + [vmem] + [pl.BlockSpec(memory_space=pl.ANY)] * len(stations),
        out_specs=[vmem] * 2,
        scratch_shapes=[pltpu.VMEM((NX, 2 * NY, BLK, days), jnp.bfloat16), pltpu.SemaphoreType.DMA((33,))],
        compiler_params=pltpu.CompilerParams(vmem_limit_bytes=VMEM_CAP),
        cost_estimate=pl.CostEstimate(flops=2 * count * BLK * BLK * days, bytes_accessed=64 * BLK * days * 2, transcendentals=0),
        name="grams",
    )(table, place, pairs, farms, *stations)


def pass_on(value, after):
    spec = pl.BlockSpec(memory_space=pl.ANY)
    return pl.pallas_call(
        lambda *refs: None,
        out_shape=jax.ShapeDtypeStruct(value.shape, value.dtype),
        in_specs=[spec] * (1 + len(after)),
        out_specs=spec,
        input_output_aliases={0: 0},
        name="pass_on",
    )(value, *after)


def standardised(farm_yield):
    rows, days = farm_yield.shape
    values = farm_yield.astype(jnp.float32)
    mean = jnp.sum(values, axis=1) / days
    offset = values - mean[:, None]
    square = jnp.sum(offset * offset, axis=1)
    state = jnp.stack([mean.reshape(-1, BLK), square.reshape(-1, BLK)])
    held = float(days)
    for hop in (CORE_SWAP, z_shift(1), z_shift(2), z_shift(4)):
        other = lax.ppermute(state, "season", hop)
        gap = other[0] - state[0]
        state = jnp.stack([
            0.5 * (state[0] + other[0]),
            state[1] + other[1] + gap * gap * (0.5 * held),
        ])
        held *= 2
    center = state[0].reshape(rows, 1)
    spread = state[1].reshape(rows, 1) / held
    scaled = ((values - center) * lax.rsqrt(spread + 1e-05)).astype(jnp.bfloat16)
    return scaled.reshape(rows // BLK, BLK, days)


def season_sum(keep, send):
    other = lax.ppermute(send, "season", CORE_SWAP)
    part = [keep[d] + other[d] for d in range(NZ)]
    half = keep.shape[1] // 2
    hop = lambda v, k: lax.ppermute(v, "season", z_shift(k))
    up4, down4 = hop(part[4][:half], 3), hop(part[4][half:], -3)
    up3, down3 = hop(part[3], 2), hop(part[5], -2)
    up2, down2 = hop(part[2], 1), hop(part[6], -1)
    right, left = part[1] + up2 + up3, part[7] + down2 + down3
    right = jnp.concatenate([right[:half] + up4, right[half:]])
    left = jnp.concatenate([left[:half], left[half:] + down4])
    total = part[0] + hop(right, 1) + hop(left, -1)
    return total.transpose(1, 0, 2)


def gates(k, relayed, farms):
    return relayed[k] if 1 <= k < 3 else []


def shards(station_index, strike_day, exit_day, farm_yield, send_list, pair_list):
    days = farm_yield.shape[1]
    all_days = days * lax.axis_size("season")
    farm, season = lax.axis_index("farm"), lax.axis_index("season")
    place = jnp.stack([farm // NY, farm % NY, season // 2, season % 2]).astype(jnp.int32)

    along = lambda v, hop: lax.ppermute(v, "farm", hop)
    wanted = send_list.reshape(NX, NY, 2).transpose(1, 0, 2)
    table = lax.all_to_all(wanted, "farm", 0, 0, axis_index_groups=ROWS, tiled=True).reshape(NY, 2 * NX)
    mine = lax.dynamic_index_in_dim(wanted, farm % NY, 0).reshape(1, 2 * NX)

    blocks = station_index.shape[0] // BLK
    start = payouts(station_index, strike_day, exit_day, 0, blocks // 2)
    own = payouts(station_index, strike_day, exit_day, blocks // 2, blocks // 2, start, table)

    farms = standardised(farm_yield)

    relayed = []

    def relay(table, sources, backs, gate=()):
        chosen = picks(table, place, sources, backs, gate)
        relayed.append([along(v, x_shift(step)) for v, step in zip(chosen, STEPS)])

    half = BLK // 2
    relay(mine, [own], (None,))
    ups, downs = [along(own, y_shift(1))], [along(own, y_shift(-1))]
    ups[0] = pass_on(ups[0], relayed[0])
    for _ in range(2):
        ups.append(along(ups[-1], y_shift(1)))
        downs.append(along(downs[-1], y_shift(-1)))
    far = [along(ups[2][:, :half], y_shift(1)), along(downs[2][:, half:], y_shift(-1))]
    for k in range(3):
        relay(table, [ups[k], downs[k]], (k + 1, NY - k - 1), gates(k, relayed, farms))
    relay(table, far, (NY // 2,), gates(3, relayed, farms))

    held = [own] + [v for k in range(3) for v in (ups[k], downs[k])] + far
    stations = held + [v for group in relayed for v in group]
    keep, send = grams(float(all_days) ** -0.5, table, place, pair_list, farms, stations)
    return season_sum(keep, send)


def solution(mesh):
    return jax.shard_map(
        shards,
        mesh=mesh,
        in_specs=(
            P("farm", "season"),
            P("farm"),
            P("farm"),
            P("farm", "season"),
            P("farm", None, None),
            P("farm", None),
        ),
        out_specs=P("season", "farm", None),
        check_vma=False,
    )
```

```python
import jax
import jax.numpy as jnp
from jax import lax
from jax.experimental import pallas as pl
from jax.experimental.pallas import tpu as pltpu
from jax.sharding import PartitionSpec as P

DAY = 128
BLK = 128
NX, NY, NZ = 4, 8, 8
FB_DEV = 8
STEPS = (2, 1, 3)
VMEM_CAP = 48 * 1024 * 1024


def y_shift(k):
    return [(x * NY + y, x * NY + (y + k) % NY) for x in range(NX) for y in range(NY)]


ROWS = [[x * NY + y for y in range(NY)] for x in range(NX)]


def x_shift(k):
    return [(x * NY + y, ((x + k) % NX) * NY + y) for x in range(NX) for y in range(NY)]


def z_shift(k):
    return [(z * 2 + c, ((z + k) % NZ) * 2 + c) for z in range(NZ) for c in range(2)]


CORE_SWAP = [(i, i ^ 1) for i in range(2 * NZ)]


def payout_kernel(strike_ref, exit_ref, series_ref, out_ref):
    b = pl.program_id(0)
    tau = lax.broadcasted_iota(jnp.int32, (BLK, DAY), 1)
    row = lax.broadcasted_iota(jnp.int32, (BLK, DAY), 0)
    upper = jnp.where(row <= tau, 1.0, 0.0).astype(jnp.bfloat16)
    tau = tau.astype(jnp.float32)

    def column(ref):
        line = ref[pl.ds(b, 1), :].astype(jnp.float32)
        return jnp.transpose(jnp.broadcast_to(line, (BLK, BLK)))

    start_on = tau >= column(strike_ref)
    window_on = start_on & (tau < column(exit_ref))
    for s in range(out_ref.shape[2] // DAY):
        days = slice(s * DAY, (s + 1) * DAY)
        x = series_ref[:, days].astype(jnp.float32)
        masked = jnp.where(start_on, x, 0.0).astype(jnp.bfloat16)
        running = jnp.dot(masked, upper, preferred_element_type=jnp.float32)
        v = 0.3 * running + x
        value = jnp.maximum(v, 0.0) + jnp.log1p(jnp.exp(-jnp.abs(v)))
        out_ref[0, :, days] = jnp.where(window_on, value, 0.0).astype(jnp.bfloat16)


def payouts(series, strike, leave):
    rows, days = series.shape
    blocks = rows // BLK
    lines = pl.BlockSpec((blocks, BLK), lambda b: (0, 0))
    return pl.pallas_call(
        payout_kernel,
        grid=(blocks,),
        out_shape=jax.ShapeDtypeStruct((blocks, BLK, days), jnp.bfloat16),
        in_specs=[lines, lines, pl.BlockSpec((BLK, days), lambda b: (b, 0))],
        out_specs=pl.BlockSpec((1, BLK, days), lambda b: (b, 0, 0)),
        name="payouts",
    )(strike.reshape(blocks, BLK), leave.reshape(blocks, BLK), series)


def pick_kernel(backs, steps, table_ref, place_ref, *refs):
    outs, held, sems = refs[-2 - len(steps):-2], refs[-2], refs[-1]
    half = BLK // 2
    copies = []
    for step, out in zip(steps, outs):
        x = lax.rem(place_ref[0] + step, NX)
        for i, back in enumerate(backs):
            line = 0 if back is None else lax.rem(place_ref[1] + NY - back, NY)
            for c in range(2):
                block = table_ref[line, (x * NY + place_ref[1]) * 2 + c]
                n, where = len(copies), out.at[2 * i + c]
                if refs[0].shape[1] == BLK:
                    copies.append((refs[i].at[block], where, n, 0, BLK))
                else:
                    for h in range(2):
                        copies.append((refs[h].at[block], where.at[pl.ds(h * half, half)], n, h * half, half))
    inward, outward = [], []
    for n, (src, dst, at, low, rows) in enumerate(copies):
        copy = pltpu.make_async_copy(src, held.at[at, pl.ds(low, rows)], sems.at[0, n])
        copy.start()
        inward.append(copy)
    for n, (src, dst, at, low, rows) in enumerate(copies):
        inward[n].wait()
        copy = pltpu.make_async_copy(held.at[at, pl.ds(low, rows)], dst, sems.at[1, n])
        copy.start()
        outward.append(copy)
    for copy in outward:
        copy.wait()


def picks(table, place, sources, backs, steps, gate=()):
    days = sources[0].shape[-1]
    count = 2 * len(backs)
    number = count * len(steps) * (1 if sources[0].shape[1] == BLK else 2)
    operands = list(sources) + list(gate)
    return pl.pallas_call(
        lambda *refs: pick_kernel(backs, steps, *refs),
        out_shape=[jax.ShapeDtypeStruct((count, BLK, days), jnp.bfloat16)] * len(steps),
        in_specs=[pl.BlockSpec(memory_space=pltpu.SMEM)] * 2 + [pl.BlockSpec(memory_space=pl.ANY)] * len(operands),
        out_specs=[pl.BlockSpec(memory_space=pl.ANY)] * len(steps),
        scratch_shapes=[pltpu.VMEM((number, BLK, days), jnp.bfloat16), pltpu.SemaphoreType.DMA((2, number))],
        compiler_params=pltpu.CompilerParams(vmem_limit_bytes=VMEM_CAP),
        cost_estimate=pl.CostEstimate(flops=0, bytes_accessed=number * BLK * days * 4, transcendentals=0),
        name="picks",
    )(table, place, *operands)


def gram_kernel(factor, table_ref, place_ref, pair_ref, farm_ref, *refs):
    held, relayed = refs[:9], refs[9:24]
    keep_ref, send_ref, slots, sems = refs[24:]
    x, y, core = place_ref[0], place_ref[1], place_ref[3]
    copies = []
    half = BLK // 2
    for at, back in enumerate((0, 1, 7, 2, 6, 3, 5, 4)):
        for c in range(2):
            block = table_ref[lax.rem(y + NY - back, NY), (x * NY + y) * 2 + c]
            if at < 7:
                copies.append((held[at].at[block], slots.at[0, 2 * at + c]))
            else:
                for h in range(2):
                    copies.append((held[7 + h].at[block], slots.at[0, 2 * at + c, pl.ds(h * half, half)]))
    for i, step in enumerate(STEPS):
        at = 0
        for ref in relayed[i::len(STEPS)]:
            n = ref.shape[0]
            copies.append((ref, slots.at[step, pl.ds(at, n)]))
            at += n
    started = []
    for n, (src, dst) in enumerate(copies):
        copy = pltpu.make_async_copy(src, dst, sems.at[n])
        copy.start()
        started.append(copy)
    for copy in started:
        copy.wait()

    first = (x * NY + y) * FB_DEV

    def one(p):
        farm = pair_ref[p, 0] - first
        slot = pair_ref[p, 1]
        source, c = slot // 2, lax.rem(slot, 2)
        sx, sy = source // NY, lax.rem(source, NY)
        dy = lax.rem(y - sy + NY, NY)
        place = jnp.where(dy == 0, 0, jnp.where(dy < 4, 2 * dy - 1, jnp.where(dy == 4, 7, 2 * (NY - dy))))
        product = lax.dot_general(
            farm_ref[farm], slots[lax.rem(x - sx + NX, NX), place * 2 + c], (((1,), (1,)), ((), ())), preferred_element_type=jnp.float32
        ) * factor
        for target in range(NZ):
            near_rows = product[target * 16: target * 16 + 8]
            far_rows = product[target * 16 + 8: target * 16 + 16]
            keep_ref[target, p] = jnp.where(core == 0, near_rows, far_rows)
            send_ref[target, p] = jnp.where(core == 0, far_rows, near_rows)

    pl.loop(0, pair_ref.shape[0], unroll=4)(one)


def grams(factor, table, place, pairs, farms, stations):
    days = farms.shape[-1]
    count = pairs.shape[0]
    shape = jax.ShapeDtypeStruct((NZ, count, 8, BLK), jnp.float32)
    vmem = pl.BlockSpec(memory_space=pltpu.VMEM)
    return pl.pallas_call(
        lambda *refs: gram_kernel(factor, *refs),
        out_shape=[shape] * 2,
        in_specs=[pl.BlockSpec(memory_space=pltpu.SMEM)] * 3 + [vmem] + [pl.BlockSpec(memory_space=pl.ANY)] * len(stations),
        out_specs=[vmem] * 2,
        scratch_shapes=[pltpu.VMEM((NX, 2 * NY, BLK, days), jnp.bfloat16), pltpu.SemaphoreType.DMA((33,))],
        compiler_params=pltpu.CompilerParams(vmem_limit_bytes=VMEM_CAP),
        cost_estimate=pl.CostEstimate(flops=2 * count * BLK * BLK * days, bytes_accessed=64 * BLK * days * 2, transcendentals=0),
        name="grams",
    )(table, place, pairs, farms, *stations)


def pass_on(values, after):
    spec = pl.BlockSpec(memory_space=pl.ANY)
    return pl.pallas_call(
        lambda *refs: None,
        out_shape=[jax.ShapeDtypeStruct(v.shape, v.dtype) for v in values],
        in_specs=[spec] * (len(values) + len(after)),
        out_specs=[spec] * len(values),
        input_output_aliases={i: i for i in range(len(values))},
        name="pass_on",
    )(*values, *after)


def standardised(farm_yield):
    steps = []
    rows, days = farm_yield.shape
    values = farm_yield.astype(jnp.float32)
    mean = jnp.sum(values, axis=1) / days
    offset = values - mean[:, None]
    square = jnp.sum(offset * offset, axis=1)
    state = jnp.stack([mean.reshape(-1, BLK), square.reshape(-1, BLK)])
    held = float(days)
    for hop in (CORE_SWAP, z_shift(1), z_shift(2), z_shift(4)):
        other = lax.ppermute(state, "season", hop)
        steps.append(other)
        gap = other[0] - state[0]
        state = jnp.stack([
            0.5 * (state[0] + other[0]),
            state[1] + other[1] + gap * gap * (0.5 * held),
        ])
        held *= 2
    center = state[0].reshape(rows, 1)
    spread = state[1].reshape(rows, 1) / held
    scaled = ((values - center) * lax.rsqrt(spread + 1e-05)).astype(jnp.bfloat16)
    return scaled.reshape(rows // BLK, BLK, days), steps


def season_sum(keep, send):
    part = keep + lax.ppermute(send, "season", CORE_SWAP)
    lines = [[2 * z + c for z in range(NZ)] for c in range(2)]
    parts = lax.all_to_all(part.astype(jnp.float16), "season", 0, 0, axis_index_groups=lines, tiled=True)
    total = jnp.sum(parts.astype(jnp.float32), axis=0)
    return total.transpose(1, 0, 2)


def shards(station_index, strike_day, exit_day, farm_yield, send_list, pair_list):
    days = farm_yield.shape[1]
    all_days = days * lax.axis_size("season")
    farm, season = lax.axis_index("farm"), lax.axis_index("season")
    place = jnp.stack([farm // NY, farm % NY, season // 2, season % 2]).astype(jnp.int32)

    along = lambda v, hop: lax.ppermute(v, "farm", hop)
    mine = send_list.reshape(1, -1)
    table = lax.all_to_all(
        jnp.broadcast_to(mine, (NY, mine.shape[1])), "farm", 0, 0, axis_index_groups=ROWS, tiled=True)
    own = payouts(station_index, strike_day, exit_day)
    own, = pass_on([own], [table])

    farms, steps = standardised(farm_yield)

    relayed = []

    def relay(table, sources, backs, gates=((), ())):
        arrived = []
        for steps, gate in zip((STEPS[:1], STEPS[1:]), gates):
            chosen = picks(table, place, sources, backs, steps, gate)
            arrived += [along(v, x_shift(step)) for v, step in zip(chosen, steps)]
        relayed.append(arrived)

    def before(also=()):
        return relayed[-1][:1] + list(also), relayed[-1][1:]

    half = BLK // 2
    relay(mine, [own], (None,))
    ups, downs = [along(own, y_shift(1))], [along(own, y_shift(-1))]
    ups[0], = pass_on([ups[0]], relayed[0] + steps[:1])
    for k in range(3):
        relay(table, [ups[k], downs[k]], (k + 1, NY - k - 1), before(steps[k:k + 1]) if k else ((), ()))
        if k < 2:
            ups.append(along(ups[k], y_shift(1)))
            downs.append(along(downs[k], y_shift(-1)))
            ups[k + 1], = pass_on([ups[k + 1]], relayed[k + 1][1:] if k == 0 else relayed[k + 1][:1])
    far = [along(ups[2][:, :half], y_shift(1)), along(downs[2][:, half:], y_shift(-1))]
    relay(table, far, (NY // 2,))

    held = [own] + [v for k in range(3) for v in (ups[k], downs[k])] + far
    stations = held + [v for group in relayed for v in group]
    keep, send = grams(float(all_days) ** -0.5, table, place, pair_list, farms, stations)
    return season_sum(keep, send)


def solution(mesh):
    return jax.shard_map(
        shards,
        mesh=mesh,
        in_specs=(
            P("farm", "season"),
            P("farm"),
            P("farm"),
            P("farm", "season"),
            P("farm", None, None),
            P("farm", None),
        ),
        out_specs=P("season", "farm", None),
        check_vma=False,
    )
```

```python
import jax
import jax.numpy as jnp
from jax import lax
from jax.experimental import pallas as pl
from jax.experimental.pallas import tpu as pltpu
from jax.sharding import PartitionSpec as P

DAY = 128
BLK = 128
NX, NY, NZ = 4, 8, 8
FB_DEV = 8
STEPS = (2, 1, 3)
VMEM_CAP = 48 * 1024 * 1024


def y_shift(k):
    return [(x * NY + y, x * NY + (y + k) % NY) for x in range(NX) for y in range(NY)]


ROWS = [[x * NY + y for y in range(NY)] for x in range(NX)]


def x_shift(k):
    return [(x * NY + y, ((x + k) % NX) * NY + y) for x in range(NX) for y in range(NY)]


def z_shift(k):
    return [(z * 2 + c, ((z + k) % NZ) * 2 + c) for z in range(NZ) for c in range(2)]


CORE_SWAP = [(i, i ^ 1) for i in range(2 * NZ)]


def payout_kernel(strike_ref, exit_ref, series_ref, out_ref):
    tau = lax.broadcasted_iota(jnp.int32, (BLK, DAY), 1)
    row = lax.broadcasted_iota(jnp.int32, (BLK, DAY), 0)
    upper = jnp.where(row <= tau, 1.0, 0.0).astype(jnp.bfloat16)
    tau = tau.astype(jnp.float32)
    count = out_ref.shape[0]
    for i in range(count):
        b = pl.program_id(0) * count + i

        def column(ref):
            line = ref[pl.ds(b, 1), :].astype(jnp.float32)
            return jnp.transpose(jnp.broadcast_to(line, (BLK, BLK)))

        start_on = tau >= column(strike_ref)
        window_on = start_on & (tau < column(exit_ref))
        for s in range(out_ref.shape[2] // DAY):
            days = slice(s * DAY, (s + 1) * DAY)
            x = series_ref[i * BLK:(i + 1) * BLK, days].astype(jnp.float32)
            masked = jnp.where(start_on, x, 0.0).astype(jnp.bfloat16)
            running = jnp.dot(masked, upper, preferred_element_type=jnp.float32)
            v = 0.3 * running + x
            value = jnp.maximum(v, 0.0) + jnp.log1p(jnp.exp(-jnp.abs(v)))
            out_ref[i, :, days] = jnp.where(window_on, value, 0.0).astype(jnp.bfloat16)


def payouts(series, strike, leave):
    rows, days = series.shape
    blocks, count = rows // BLK, 4
    lines = pl.BlockSpec((blocks, BLK), lambda b: (0, 0))
    return pl.pallas_call(
        payout_kernel,
        grid=(blocks // count,),
        out_shape=jax.ShapeDtypeStruct((blocks, BLK, days), jnp.bfloat16),
        in_specs=[lines, lines, pl.BlockSpec((count * BLK, days), lambda b: (b, 0))],
        out_specs=pl.BlockSpec((count, BLK, days), lambda b: (b, 0, 0)),
        name="payouts",
    )(strike.reshape(blocks, BLK), leave.reshape(blocks, BLK), series)


def pick_kernel(backs, steps, table_ref, place_ref, *refs):
    outs, held, sems = refs[-2 - len(steps):-2], refs[-2], refs[-1]
    half = BLK // 2
    copies = []
    for step, out in zip(steps, outs):
        x = lax.rem(place_ref[0] + step, NX)
        for i, back in enumerate(backs):
            line = 0 if back is None else lax.rem(place_ref[1] + NY - back, NY)
            for c in range(2):
                block = table_ref[line, (x * NY + place_ref[1]) * 2 + c]
                n, where = len(copies), out.at[2 * i + c]
                if refs[0].shape[1] == BLK:
                    copies.append((refs[i].at[block], where, n, 0, BLK))
                else:
                    for h in range(2):
                        copies.append((refs[h].at[block], where.at[pl.ds(h * half, half)], n, h * half, half))
    inward, outward = [], []
    for n, (src, dst, at, low, rows) in enumerate(copies):
        copy = pltpu.make_async_copy(src, held.at[at, pl.ds(low, rows)], sems.at[0, n])
        copy.start()
        inward.append(copy)
    for n, (src, dst, at, low, rows) in enumerate(copies):
        inward[n].wait()
        copy = pltpu.make_async_copy(held.at[at, pl.ds(low, rows)], dst, sems.at[1, n])
        copy.start()
        outward.append(copy)
    for copy in outward:
        copy.wait()


def picks(table, place, sources, backs, steps, gate=()):
    days = sources[0].shape[-1]
    count = 2 * len(backs)
    number = count * len(steps) * (1 if sources[0].shape[1] == BLK else 2)
    operands = list(sources) + list(gate)
    return pl.pallas_call(
        lambda *refs: pick_kernel(backs, steps, *refs),
        out_shape=[jax.ShapeDtypeStruct((count, BLK, days), jnp.bfloat16)] * len(steps),
        in_specs=[pl.BlockSpec(memory_space=pltpu.SMEM)] * 2 + [pl.BlockSpec(memory_space=pl.ANY)] * len(operands),
        out_specs=[pl.BlockSpec(memory_space=pl.ANY)] * len(steps),
        scratch_shapes=[pltpu.VMEM((number, BLK, days), jnp.bfloat16), pltpu.SemaphoreType.DMA((2, number))],
        compiler_params=pltpu.CompilerParams(vmem_limit_bytes=VMEM_CAP),
        cost_estimate=pl.CostEstimate(flops=0, bytes_accessed=number * BLK * days * 4, transcendentals=0),
        name="picks",
    )(table, place, *operands)


def gram_kernel(factor, table_ref, place_ref, pair_ref, farm_ref, *refs):
    held, relayed = refs[:9], refs[9:24]
    keep_ref, send_ref, slots, sems = refs[24:]
    x, y, core = place_ref[0], place_ref[1], place_ref[3]
    copies = []
    half = BLK // 2
    for at, back in enumerate((0, 1, 7, 2, 6, 3, 5, 4)):
        for c in range(2):
            block = table_ref[lax.rem(y + NY - back, NY), (x * NY + y) * 2 + c]
            if at < 7:
                copies.append((held[at].at[block], slots.at[0, 2 * at + c]))
            else:
                for h in range(2):
                    copies.append((held[7 + h].at[block], slots.at[0, 2 * at + c, pl.ds(h * half, half)]))
    for i, step in enumerate(STEPS):
        at = 0
        for ref in relayed[i::len(STEPS)]:
            n = ref.shape[0]
            copies.append((ref, slots.at[step, pl.ds(at, n)]))
            at += n
    started = []
    for n, (src, dst) in enumerate(copies):
        copy = pltpu.make_async_copy(src, dst, sems.at[n])
        copy.start()
        started.append(copy)
    for copy in started:
        copy.wait()

    first = (x * NY + y) * FB_DEV

    def one(p):
        farm = pair_ref[p, 0] - first
        slot = pair_ref[p, 1]
        source, c = slot // 2, lax.rem(slot, 2)
        sx, sy = source // NY, lax.rem(source, NY)
        dy = lax.rem(y - sy + NY, NY)
        place = jnp.where(dy == 0, 0, jnp.where(dy < 4, 2 * dy - 1, jnp.where(dy == 4, 7, 2 * (NY - dy))))
        product = lax.dot_general(
            farm_ref[farm], slots[lax.rem(x - sx + NX, NX), place * 2 + c], (((1,), (1,)), ((), ())), preferred_element_type=jnp.float32
        ) * factor
        for target in range(NZ):
            near_rows = product[target * 16: target * 16 + 8]
            far_rows = product[target * 16 + 8: target * 16 + 16]
            keep_ref[target, p] = jnp.where(core == 0, near_rows, far_rows)
            send_ref[target, p] = jnp.where(core == 0, far_rows, near_rows)

    pl.loop(0, pair_ref.shape[0], unroll=8)(one)


def grams(factor, table, place, pairs, farms, stations):
    days = farms.shape[-1]
    count = pairs.shape[0]
    shape = jax.ShapeDtypeStruct((NZ, count, 8, BLK), jnp.float32)
    vmem = pl.BlockSpec(memory_space=pltpu.VMEM)
    return pl.pallas_call(
        lambda *refs: gram_kernel(factor, *refs),
        out_shape=[shape] * 2,
        in_specs=[pl.BlockSpec(memory_space=pltpu.SMEM)] * 3 + [vmem] + [pl.BlockSpec(memory_space=pl.ANY)] * len(stations),
        out_specs=[vmem] * 2,
        scratch_shapes=[pltpu.VMEM((NX, 2 * NY, BLK, days), jnp.bfloat16), pltpu.SemaphoreType.DMA((33,))],
        compiler_params=pltpu.CompilerParams(vmem_limit_bytes=VMEM_CAP),
        cost_estimate=pl.CostEstimate(flops=2 * count * BLK * BLK * days, bytes_accessed=64 * BLK * days * 2, transcendentals=0),
        name="grams",
    )(table, place, pairs, farms, *stations)


def pass_on(values, after):
    spec = pl.BlockSpec(memory_space=pl.ANY)
    return pl.pallas_call(
        lambda *refs: None,
        out_shape=[jax.ShapeDtypeStruct(v.shape, v.dtype) for v in values],
        in_specs=[spec] * (len(values) + len(after)),
        out_specs=[spec] * len(values),
        input_output_aliases={i: i for i in range(len(values))},
        name="pass_on",
    )(*values, *after)


def standardised(farm_yield):
    steps = []
    rows, days = farm_yield.shape
    values = farm_yield.astype(jnp.float32)
    mean = jnp.sum(values, axis=1) / days
    offset = values - mean[:, None]
    square = jnp.sum(offset * offset, axis=1)
    state = jnp.stack([mean.reshape(-1, BLK), square.reshape(-1, BLK)])
    held = float(days)
    for hop in (CORE_SWAP, z_shift(1), z_shift(2), z_shift(4)):
        other = lax.ppermute(state, "season", hop)
        steps.append(other)
        gap = other[0] - state[0]
        state = jnp.stack([
            0.5 * (state[0] + other[0]),
            state[1] + other[1] + gap * gap * (0.5 * held),
        ])
        held *= 2
    center = state[0].reshape(rows, 1)
    spread = state[1].reshape(rows, 1) / held
    scaled = ((values - center) * lax.rsqrt(spread + 1e-05)).astype(jnp.bfloat16)
    return scaled.reshape(rows // BLK, BLK, days), steps


def season_sum(keep, send):
    part = keep + lax.ppermute(send, "season", CORE_SWAP)
    lines = [[2 * z + c for z in range(NZ)] for c in range(2)]
    parts = lax.all_to_all(part.astype(jnp.float16), "season", 0, 0, axis_index_groups=lines, tiled=True)
    total = jnp.sum(parts.astype(jnp.float32), axis=0)
    return total.transpose(1, 0, 2)


def shards(station_index, strike_day, exit_day, farm_yield, send_list, pair_list):
    days = farm_yield.shape[1]
    all_days = days * lax.axis_size("season")
    farm, season = lax.axis_index("farm"), lax.axis_index("season")
    place = jnp.stack([farm // NY, farm % NY, season // 2, season % 2]).astype(jnp.int32)

    along = lambda v, hop: lax.ppermute(v, "farm", hop)
    mine = send_list.reshape(1, -1)
    table = lax.all_to_all(
        jnp.broadcast_to(mine, (NY, mine.shape[1])), "farm", 0, 0, axis_index_groups=ROWS, tiled=True)
    own = payouts(station_index, strike_day, exit_day)
    own, = pass_on([own], [table])

    farms, steps = standardised(farm_yield)

    relayed = []

    def relay(table, sources, backs, gates=((), ())):
        arrived = []
        for steps, gate in zip((STEPS[:1], STEPS[1:]), gates):
            chosen = picks(table, place, sources, backs, steps, gate)
            arrived += [along(v, x_shift(step)) for v, step in zip(chosen, steps)]
        relayed.append(arrived)

    def before(also=()):
        return relayed[-1][:1] + list(also), relayed[-1][1:]

    half = BLK // 2
    relay(mine, [own], (None,))
    ups, downs = [along(own, y_shift(1))], [along(own, y_shift(-1))]
    ups[0], = pass_on([ups[0]], relayed[0] + steps[:1])
    for k in range(3):
        relay(table, [ups[k], downs[k]], (k + 1, NY - k - 1), before(steps[k:k + 1]) if k else ((), ()))
        if k < 2:
            ups.append(along(ups[k], y_shift(1)))
            downs.append(along(downs[k], y_shift(-1)))
            ups[k + 1], = pass_on([ups[k + 1]], relayed[k + 1][1:] if k == 0 else relayed[k + 1][:1])
    far = [along(ups[2][:, :half], y_shift(1)), along(downs[2][:, half:], y_shift(-1))]
    relay(table, far, (NY // 2,))

    held = [own] + [v for k in range(3) for v in (ups[k], downs[k])] + far
    stations = held + [v for group in relayed for v in group]
    keep, send = grams(float(all_days) ** -0.5, table, place, pair_list, farms, stations)
    return season_sum(keep, send)


def solution(mesh):
    return jax.shard_map(
        shards,
        mesh=mesh,
        in_specs=(
            P("farm", "season"),
            P("farm"),
            P("farm"),
            P("farm", "season"),
            P("farm", None, None),
            P("farm", None),
        ),
        out_specs=P("season", "farm", None),
        check_vma=False,
    )
```

```python
import jax
import jax.numpy as jnp
from jax import lax
from jax.experimental import pallas as pl
from jax.experimental.pallas import tpu as pltpu
from jax.sharding import PartitionSpec as P

DAY = 128
BLK = 128
NX, NY, NZ = 4, 8, 8
FB_DEV = 8
STEPS = (2, 1, 3)
VMEM_CAP = 48 * 1024 * 1024


def y_shift(k):
    return [(x * NY + y, x * NY + (y + k) % NY) for x in range(NX) for y in range(NY)]


ROWS = [[x * NY + y for y in range(NY)] for x in range(NX)]


def x_shift(k):
    return [(x * NY + y, ((x + k) % NX) * NY + y) for x in range(NX) for y in range(NY)]


def z_shift(k):
    return [(z * 2 + c, ((z + k) % NZ) * 2 + c) for z in range(NZ) for c in range(2)]


CORE_SWAP = [(i, i ^ 1) for i in range(2 * NZ)]


def payout_kernel(strike_ref, exit_ref, series_ref, out_ref):
    tau = lax.broadcasted_iota(jnp.int32, (BLK, DAY), 1)
    row = lax.broadcasted_iota(jnp.int32, (BLK, DAY), 0)
    upper = jnp.where(row <= tau, 1.0, 0.0).astype(jnp.bfloat16)
    tau = tau.astype(jnp.float32)
    count = out_ref.shape[0]
    for i in range(count):
        b = pl.program_id(0) * count + i

        def column(ref):
            line = ref[pl.ds(b, 1), :].astype(jnp.float32)
            return jnp.transpose(jnp.broadcast_to(line, (BLK, BLK)))

        start_on = tau >= column(strike_ref)
        window_on = start_on & (tau < column(exit_ref))
        for s in range(out_ref.shape[2] // DAY):
            days = slice(s * DAY, (s + 1) * DAY)
            x = series_ref[i * BLK:(i + 1) * BLK, days].astype(jnp.float32)
            masked = jnp.where(start_on, x, 0.0).astype(jnp.bfloat16)
            running = jnp.dot(masked, upper, preferred_element_type=jnp.float32)
            v = 0.3 * running + x
            value = jnp.maximum(v, 0.0) + jnp.log1p(jnp.exp(-jnp.abs(v)))
            out_ref[i, :, days] = jnp.where(window_on, value, 0.0).astype(jnp.bfloat16)


def payouts(series, strike, leave):
    rows, days = series.shape
    blocks, count = rows // BLK, 4
    lines = pl.BlockSpec((blocks, BLK), lambda b: (0, 0))
    return pl.pallas_call(
        payout_kernel,
        grid=(blocks // count,),
        out_shape=jax.ShapeDtypeStruct((blocks, BLK, days), jnp.bfloat16),
        in_specs=[lines, lines, pl.BlockSpec((count * BLK, days), lambda b: (b, 0))],
        out_specs=pl.BlockSpec((count, BLK, days), lambda b: (b, 0, 0)),
        name="payouts",
    )(strike.reshape(blocks, BLK), leave.reshape(blocks, BLK), series)


def pick_kernel(backs, steps, table_ref, place_ref, *refs):
    outs, held, sems = refs[-2 - len(steps):-2], refs[-2], refs[-1]
    half = BLK // 2
    copies = []
    for step, out in zip(steps, outs):
        x = lax.rem(place_ref[0] + step, NX)
        for i, back in enumerate(backs):
            line = 0 if back is None else lax.rem(place_ref[1] + NY - back, NY)
            for c in range(2):
                block = table_ref[line, (x * NY + place_ref[1]) * 2 + c]
                n, where = len(copies), out.at[2 * i + c]
                if refs[0].shape[1] == BLK:
                    copies.append((refs[i].at[block], where, n, 0, BLK))
                else:
                    for h in range(2):
                        copies.append((refs[h].at[block], where.at[pl.ds(h * half, half)], n, h * half, half))
    inward, outward = [], []
    for n, (src, dst, at, low, rows) in enumerate(copies):
        copy = pltpu.make_async_copy(src, held.at[at, pl.ds(low, rows)], sems.at[0, n])
        copy.start()
        inward.append(copy)
    for n, (src, dst, at, low, rows) in enumerate(copies):
        inward[n].wait()
        copy = pltpu.make_async_copy(held.at[at, pl.ds(low, rows)], dst, sems.at[1, n])
        copy.start()
        outward.append(copy)
    for copy in outward:
        copy.wait()


def picks(table, place, sources, backs, steps, gate=()):
    days = sources[0].shape[-1]
    count = 2 * len(backs)
    number = count * len(steps) * (1 if sources[0].shape[1] == BLK else 2)
    operands = list(sources) + list(gate)
    return pl.pallas_call(
        lambda *refs: pick_kernel(backs, steps, *refs),
        out_shape=[jax.ShapeDtypeStruct((count, BLK, days), jnp.bfloat16)] * len(steps),
        in_specs=[pl.BlockSpec(memory_space=pltpu.SMEM)] * 2 + [pl.BlockSpec(memory_space=pl.ANY)] * len(operands),
        out_specs=[pl.BlockSpec(memory_space=pl.ANY)] * len(steps),
        scratch_shapes=[pltpu.VMEM((number, BLK, days), jnp.bfloat16), pltpu.SemaphoreType.DMA((2, number))],
        compiler_params=pltpu.CompilerParams(vmem_limit_bytes=VMEM_CAP),
        cost_estimate=pl.CostEstimate(flops=0, bytes_accessed=number * BLK * days * 4, transcendentals=0),
        name="picks",
    )(table, place, *operands)


def gram_kernel(factor, table_ref, place_ref, pair_ref, farm_ref, *refs):
    held, relayed = refs[:9], refs[9:24]
    keep_ref, send_ref, slots, sems = refs[24:]
    x, y, core = place_ref[0], place_ref[1], place_ref[3]
    copies = []
    half = BLK // 2
    for at, back in enumerate((0, 1, 7, 2, 6, 3, 5, 4)):
        for c in range(2):
            block = table_ref[lax.rem(y + NY - back, NY), (x * NY + y) * 2 + c]
            if at < 7:
                copies.append((held[at].at[block], slots.at[0, 2 * at + c]))
            else:
                for h in range(2):
                    copies.append((held[7 + h].at[block], slots.at[0, 2 * at + c, pl.ds(h * half, half)]))
    for i, step in enumerate(STEPS):
        at = 0
        for ref in relayed[i::len(STEPS)]:
            n = ref.shape[0]
            copies.append((ref, slots.at[step, pl.ds(at, n)]))
            at += n
    started = []
    for n, (src, dst) in enumerate(copies):
        copy = pltpu.make_async_copy(src, dst, sems.at[n])
        copy.start()
        started.append(copy)
    for copy in started:
        copy.wait()

    first = (x * NY + y) * FB_DEV

    def one(p):
        farm = pair_ref[p, 0] - first
        slot = pair_ref[p, 1]
        source, c = slot // 2, lax.rem(slot, 2)
        sx, sy = source // NY, lax.rem(source, NY)
        dy = lax.rem(y - sy + NY, NY)
        place = jnp.where(dy == 0, 0, jnp.where(dy < 4, 2 * dy - 1, jnp.where(dy == 4, 7, 2 * (NY - dy))))
        product = lax.dot_general(
            farm_ref[farm], slots[lax.rem(x - sx + NX, NX), place * 2 + c], (((1,), (1,)), ((), ())), preferred_element_type=jnp.float32
        ) * factor
        for target in range(NZ):
            near_rows = product[target * 16: target * 16 + 8]
            far_rows = product[target * 16 + 8: target * 16 + 16]
            keep_ref[target, p] = jnp.where(core == 0, near_rows, far_rows)
            send_ref[target, p] = jnp.where(core == 0, far_rows, near_rows)

    pl.loop(0, pair_ref.shape[0], unroll=16)(one)


def grams(factor, table, place, pairs, farms, stations):
    days = farms.shape[-1]
    count = pairs.shape[0]
    shape = jax.ShapeDtypeStruct((NZ, count, 8, BLK), jnp.float32)
    vmem = pl.BlockSpec(memory_space=pltpu.VMEM)
    return pl.pallas_call(
        lambda *refs: gram_kernel(factor, *refs),
        out_shape=[shape] * 2,
        in_specs=[pl.BlockSpec(memory_space=pltpu.SMEM)] * 3 + [vmem] + [pl.BlockSpec(memory_space=pl.ANY)] * len(stations),
        out_specs=[vmem] * 2,
        scratch_shapes=[pltpu.VMEM((NX, 2 * NY, BLK, days), jnp.bfloat16), pltpu.SemaphoreType.DMA((33,))],
        compiler_params=pltpu.CompilerParams(vmem_limit_bytes=VMEM_CAP),
        cost_estimate=pl.CostEstimate(flops=2 * count * BLK * BLK * days, bytes_accessed=64 * BLK * days * 2, transcendentals=0),
        name="grams",
    )(table, place, pairs, farms, *stations)


def pass_on(values, after):
    spec = pl.BlockSpec(memory_space=pl.ANY)
    return pl.pallas_call(
        lambda *refs: None,
        out_shape=[jax.ShapeDtypeStruct(v.shape, v.dtype) for v in values],
        in_specs=[spec] * (len(values) + len(after)),
        out_specs=[spec] * len(values),
        input_output_aliases={i: i for i in range(len(values))},
        name="pass_on",
    )(*values, *after)


def standardised(farm_yield):
    steps = []
    rows, days = farm_yield.shape
    values = farm_yield.astype(jnp.float32)
    mean = jnp.sum(values, axis=1) / days
    offset = values - mean[:, None]
    square = jnp.sum(offset * offset, axis=1)
    state = jnp.stack([mean.reshape(-1, BLK), square.reshape(-1, BLK)])
    held = float(days)
    for hop in (CORE_SWAP, z_shift(1), z_shift(2), z_shift(4)):
        other = lax.ppermute(state, "season", hop)
        steps.append(other)
        gap = other[0] - state[0]
        state = jnp.stack([
            0.5 * (state[0] + other[0]),
            state[1] + other[1] + gap * gap * (0.5 * held),
        ])
        held *= 2
    center = state[0].reshape(rows, 1)
    spread = state[1].reshape(rows, 1) / held
    scaled = ((values - center) * lax.rsqrt(spread + 1e-05)).astype(jnp.bfloat16)
    return scaled.reshape(rows // BLK, BLK, days), steps


def season_sum(keep, send):
    part = keep + lax.ppermute(send, "season", CORE_SWAP)
    lines = [[2 * z + c for z in range(NZ)] for c in range(2)]
    parts = lax.all_to_all(part.astype(jnp.float16), "season", 0, 0, axis_index_groups=lines, tiled=True)
    total = jnp.sum(parts.astype(jnp.float32), axis=0)
    return total.transpose(1, 0, 2)


def shards(station_index, strike_day, exit_day, farm_yield, send_list, pair_list):
    days = farm_yield.shape[1]
    all_days = days * lax.axis_size("season")
    farm, season = lax.axis_index("farm"), lax.axis_index("season")
    place = jnp.stack([farm // NY, farm % NY, season // 2, season % 2]).astype(jnp.int32)

    along = lambda v, hop: lax.ppermute(v, "farm", hop)
    mine = send_list.reshape(1, -1)
    table = lax.all_to_all(
        jnp.broadcast_to(mine, (NY, mine.shape[1])), "farm", 0, 0, axis_index_groups=ROWS, tiled=True)
    own = payouts(station_index, strike_day, exit_day)
    own, = pass_on([own], [table])

    farms, steps = standardised(farm_yield)

    relayed = []

    def relay(table, sources, backs, gates=((), ())):
        arrived = []
        for steps, gate in zip((STEPS[:1], STEPS[1:]), gates):
            chosen = picks(table, place, sources, backs, steps, gate)
            arrived += [along(v, x_shift(step)) for v, step in zip(chosen, steps)]
        relayed.append(arrived)

    def before(also=()):
        return relayed[-1][:1] + list(also), relayed[-1][1:]

    half = BLK // 2
    relay(mine, [own], (None,))
    ups, downs = [along(own, y_shift(1))], [along(own, y_shift(-1))]
    ups[0], = pass_on([ups[0]], relayed[0] + steps[:1])
    for k in range(3):
        relay(table, [ups[k], downs[k]], (k + 1, NY - k - 1), before(steps[k:k + 1]) if k else ((), ()))
        if k < 2:
            ups.append(along(ups[k], y_shift(1)))
            downs.append(along(downs[k], y_shift(-1)))
            ups[k + 1], = pass_on([ups[k + 1]], relayed[k + 1][1:] if k == 0 else relayed[k + 1][:1])
    far = [along(ups[2][:, :half], y_shift(1)), along(downs[2][:, half:], y_shift(-1))]
    relay(table, far, (NY // 2,))

    held = [own] + [v for k in range(3) for v in (ups[k], downs[k])] + far
    stations = held + [v for group in relayed for v in group]
    keep, send = grams(float(all_days) ** -0.5, table, place, pair_list, farms, stations)
    return season_sum(keep, send)


def solution(mesh):
    return jax.shard_map(
        shards,
        mesh=mesh,
        in_specs=(
            P("farm", "season"),
            P("farm"),
            P("farm"),
            P("farm", "season"),
            P("farm", None, None),
            P("farm", None),
        ),
        out_specs=P("season", "farm", None),
        check_vma=False,
    )
```
